512 devices in a mesh: grp: 16 (over x, y_hi, core), seq: 32 (over z, y_lo).
Axes of the slice: x: 4, y: 4 (y_hi: 2, y_lo: 2; y = y_hi * 2 + y_lo), z: 16, core: 2. Of those that a mesh axis runs over, the one named last changes fastest.
Arguments:
- query_vectors: bfloat16 [512, 256, 2048], P(('grp', 'seq')), parts along dimension 0, may hold values from -4000 to 4000
- key_vectors: bfloat16 [512, 256, 2048], P(('grp', 'seq')), parts along dimension 0, may hold values from -6 to 6
- value_vectors: bfloat16 [512, 256, 2048], P(('grp', 'seq')), parts along dimension 0, may hold values from -6 to 6
Outputs:
- attended: bfloat16 [512, 256, 2048], P(('grp', 'seq')), parts along dimension 0
The draws below stay inside these ranges and needn't reach their ends.
There are 16 independent parts, one for each index of `grp`. The reference program is written for one: setup_inputs(seed, part) draws one part's arguments, and reference() takes and returns one part's arrays. A program takes and returns all parts, laid end to end along the dimension named above; each array names one. Nothing has to cross between parts.
All inputs are finite; a program needn't handle non-finite values.
Results may differ from the reference program's by a relative error of at most 0.0065.
Values may be sent and summed in bfloat16 or wider, within the bound.
A program may use at most 64 MiB of HBM per device.

```python
import math
import jax
import jax.numpy as jnp
from jax import lax

HEADS = 16
HD = 128
COLS = 256
ROWS = 32


def draw_query_vectors(key, part):
    key = jax.random.fold_in(key, 11)
    sample = jnp.clip(jax.random.normal(key, (ROWS, COLS, HEADS, HD), jnp.float32), -6.0, 6.0)
    return sample.reshape(ROWS, COLS, HEADS * HD).astype(jnp.bfloat16)


def draw_key_vectors(key, part):
    key = jax.random.fold_in(key, 23)
    sample = jnp.clip(jax.random.normal(key, (ROWS, COLS, HEADS, HD), jnp.float32), -6.0, 6.0)
    return sample.reshape(ROWS, COLS, HEADS * HD).astype(jnp.bfloat16)


def block_scale(rng, dims, pieces, low, largest):
    def one(dim, parts):
        heights = jax.random.uniform(jax.random.fold_in(jax.random.fold_in(rng, 6), dim), (parts,), jnp.float32, low / len(pieces), largest / len(pieces))
        return jnp.repeat(jnp.exp(heights), dims[dim] // parts).reshape((-1,) + (1,) * (len(dims) - dim - 1))

    factor_of = one(*pieces[0])
    for cut in pieces[1:]:
        factor_of = factor_of * one(*cut)
    return factor_of


def centred(own_key, shape, scale, bound, shards=(), held_as=jnp.bfloat16):
    gain = block_scale(own_key, shape, shards, -0.22, 0.18) if shards else 1.0
    result = jax.random.normal(own_key, shape, jnp.float32) * scale * gain
    return jnp.minimum(jnp.maximum(result, -bound), bound).astype(held_as)


def setup_inputs(seed: int = 0, part: int = 0) -> dict:
    streams_of = jax.random.split(jax.random.key(seed), 4)
    own_keys = jax.random.split(jax.random.fold_in(streams_of[3], part), 4)
    query_vectors = draw_query_vectors(jax.random.fold_in(jax.random.fold_in(streams_of[3], part), 71), part)
    key_vectors = draw_key_vectors(jax.random.fold_in(jax.random.fold_in(streams_of[3], part), 71), part)
    value_vectors = centred(own_keys[2], (ROWS, COLS, HEADS * HD), 1.0, 6.0, ((0, 32),))
    return {"query_vectors": query_vectors, "key_vectors": key_vectors, "value_vectors": value_vectors}


floor_score = -1e+30

def attend(query_vectors, key_vectors, value_vectors, allowed, layout):
    shape = query_vectors.shape
    split = (shape[0], shape[1], HEADS, HD)
    query_heads = query_vectors.reshape(split).astype(jnp.float32)
    key_heads = key_vectors.reshape(split).astype(jnp.float32)
    value_heads = value_vectors.reshape(split).astype(jnp.float32)
    if layout == 'rows':
        score_form, blend_form, order = ('rahd,rbhd->rhab', 'rhab,rbhd->rahd', (0, 2, 1))
    else:
        score_form, blend_form, order = ('arhd,brhd->rhab', 'rhab,brhd->arhd', (2, 0, 1))
    scores = jnp.einsum(score_form, query_heads, key_heads) * (1.0 / math.sqrt(HD))
    scores = jnp.where(allowed, scores, floor_score)
    highest = lax.optimization_barrier(jnp.max(scores, axis=3))
    weights = jnp.where(allowed, jnp.exp(scores - highest[..., None]), 0.0)
    totals = lax.optimization_barrier(jnp.sum(weights, axis=3))
    rounded = weights.astype(jnp.bfloat16).astype(jnp.float32)
    blend = jnp.einsum(blend_form, rounded, value_heads)
    return (blend.reshape(shape).astype(jnp.bfloat16), jnp.transpose(highest, order), jnp.transpose(totals, order))

def combine_parts(row_out, row_high, row_total, col_out, col_high, col_total):
    highest = jnp.maximum(row_high, col_high)
    row_factor = jnp.exp(row_high - highest)
    col_factor = jnp.exp(col_high - highest)
    split = row_out.shape[:-1] + (HEADS, HD)
    numer = row_out.astype(jnp.float32).reshape(split) * row_factor[..., None]
    numer = numer + col_out.astype(jnp.float32).reshape(split) * col_factor[..., None]
    denom = row_total * row_factor + col_total * col_factor
    return (numer / denom[..., None]).reshape(row_out.shape).astype(jnp.bfloat16)

def reference(query_vectors, key_vectors, value_vectors):
    col_index = jnp.arange(COLS, dtype=jnp.int32)
    row_allowed = col_index[None, :] <= col_index[:, None]
    row_index = jnp.arange(ROWS, dtype=jnp.int32)
    col_allowed = row_index[None, :] < row_index[:, None]
    row_out, row_high, row_total = attend(query_vectors, key_vectors, value_vectors, row_allowed, 'rows')
    col_out, col_high, col_total = attend(query_vectors, key_vectors, value_vectors, col_allowed, 'cols')
    col_out = jnp.swapaxes(jnp.swapaxes(col_out, 0, 1), 0, 1)
    return combine_parts(row_out, row_high, row_total, col_out, col_high, col_total)
```

```python
import functools
import math

import jax
import jax.numpy as jnp
from jax import lax
from jax.experimental import pallas as pl
from jax.experimental.pallas import tpu as pltpu
from jax.sharding import PartitionSpec as P

HEADS = 16
HD = 128
FLOOR = -1e30
POWER = math.log2(math.e) / math.sqrt(HD)
CHUNK_HEADS = 4
MESH = pl.DeviceIdType.MESH


def attend(queries, keys, values, bias):
    scores = lax.dot_general(
        queries, keys, (((1,), (1,)), ((), ())), preferred_element_type=jnp.float32
    )
    scores = scores + bias
    high = jnp.max(scores, axis=1, keepdims=True)
    weights = jnp.exp2((scores - high) * POWER)
    total = jnp.sum(weights, axis=1, keepdims=True)
    out = jnp.dot(weights.astype(jnp.bfloat16), values, preferred_element_type=jnp.float32)
    return out, high, total


def kernel(
    n, cols,
    q_ref, k_ref, v_ref, out_ref,
    q_all, k_all, v_all, back, home, row_out, row_stats, col_stats, home_stats, row_bias, col_bias,
    send_sem, recv_sem, back_send, back_recv, stat_send, stat_recv, own_sem,
):
    me = lax.axis_index("seq")
    width = CHUNK_HEADS * HD
    chunks = HEADS // CHUNK_HEADS
    tokens = n * cols
    forward = ((q_ref, q_all), (k_ref, k_all), (v_ref, v_all))

    def peer(step):
        return lax.rem(me + step, n)

    barrier = pltpu.get_barrier_semaphore()

    def greet(step, carry):
        pl.semaphore_signal(
            barrier, inc=1, device_id={"seq": peer(step)}, device_id_type=MESH
        )
        return carry

    lax.fori_loop(1, n, greet, 0)

    own = [
        pltpu.make_async_copy(src.at[me], dst.at[me], own_sem.at[i])
        for i, (src, dst) in enumerate(forward)
    ]
    for copy in own:
        copy.start()

    index = lax.broadcasted_iota(jnp.int32, (tokens, tokens), 0)
    other = lax.broadcasted_iota(jnp.int32, (tokens, tokens), 1)
    row_bias[...] = jnp.where(other <= index, 0.0, FLOOR)
    same = lax.rem(index, cols) == lax.rem(other, cols)
    before = lax.div(other, cols) < lax.div(index, cols)
    col_bias[...] = jnp.where(same & before, 0.0, FLOOR)

    pl.semaphore_wait(barrier, n - 1)

    def lanes(chunk):
        return pl.ds(chunk * width, width)

    def send_chunk(chunk):
        def send(step, carry):
            to = peer(step)
            for i, (src, dst) in enumerate(forward):
                pltpu.make_async_remote_copy(
                    src_ref=src.at[to, :, lanes(chunk)],
                    dst_ref=dst.at[me, :, lanes(chunk)],
                    send_sem=send_sem.at[chunk, i],
                    recv_sem=recv_sem.at[chunk, i],
                    device_id={"seq": to},
                    device_id_type=MESH,
                ).start()
            return carry

        lax.fori_loop(1, n, send, 0)

    def chunk_copies(chunk):
        return [
            pltpu.make_async_remote_copy(
                src_ref=src.at[pl.ds(0, n - 1), :, lanes(chunk)],
                dst_ref=dst.at[pl.ds(0, n - 1), :, lanes(chunk)],
                send_sem=send_sem.at[chunk, i],
                recv_sem=recv_sem.at[chunk, i],
                device_id={"seq": peer(1)},
                device_id_type=MESH,
            )
            for i, (src, dst) in enumerate(forward)
        ]

    def back_copies(chunk):
        return pltpu.make_async_remote_copy(
            src_ref=back.at[pl.ds(0, n - 1), :, lanes(chunk)],
            dst_ref=home.at[pl.ds(0, n - 1), :, lanes(chunk)],
            send_sem=back_send.at[chunk],
            recv_sem=back_recv.at[chunk],
            device_id={"seq": peer(1)},
            device_id_type=MESH,
        )

    lane = lax.broadcasted_iota(jnp.int32, (tokens, HD), 1)

    def keep(stats, head, high, total):
        stats[...] = jnp.where(
            lane == head, high, jnp.where(lane == head + HEADS, total, stats[...])
        )

    def row_chunk(chunk):
        for sub in range(CHUNK_HEADS):
            head = chunk * CHUNK_HEADS + sub
            at = pl.ds(head * HD, HD)
            out, high, total = attend(
                q_ref[:, :, at].reshape(tokens, HD),
                k_ref[:, :, at].reshape(tokens, HD),
                v_ref[:, :, at].reshape(tokens, HD),
                row_bias[...],
            )
            row_out[:, at] = out.astype(jnp.bfloat16)
            keep(row_stats, head, high, total)

    def col_chunk(chunk):
        for sub in range(CHUNK_HEADS):
            head = chunk * CHUNK_HEADS + sub
            at = pl.ds(head * HD, HD)
            out, high, total = attend(
                q_all[:, :, at].reshape(tokens, HD),
                k_all[:, :, at].reshape(tokens, HD),
                v_all[:, :, at].reshape(tokens, HD),
                col_bias[...],
            )
            back[:, :, at] = out.astype(jnp.bfloat16).reshape(n, cols, HD)
            keep(col_stats, head, high, total)

    row_stats[...] = jnp.zeros_like(row_stats)
    col_stats[...] = jnp.zeros_like(col_stats)

    for chunk in range(chunks):
        send_chunk(chunk)

    def row_step(chunk, carry):
        row_chunk(chunk)
        return carry

    lax.fori_loop(0, chunks, row_step, 0)

    for copy in own:
        copy.wait()

    def col_step(chunk, carry):
        for copy in chunk_copies(chunk):
            copy.wait_recv()
        col_chunk(chunk)

        def send_back(step, inner):
            to = peer(step)
            pltpu.make_async_remote_copy(
                src_ref=back.at[to, :, lanes(chunk)],
                dst_ref=home.at[me, :, lanes(chunk)],
                send_sem=back_send.at[chunk],
                recv_sem=back_recv.at[chunk],
                device_id={"seq": to},
                device_id_type=MESH,
            ).start()
            return inner

        lax.fori_loop(1, n, send_back, 0)
        return carry

    lax.fori_loop(0, chunks, col_step, 0)


    def send_stats(step, carry):
        to = peer(step)
        pltpu.make_async_remote_copy(
            src_ref=col_stats.at[pl.ds(pl.multiple_of(to * cols, cols), cols)],
            dst_ref=home_stats.at[pl.ds(pl.multiple_of(me * cols, cols), cols)],
            send_sem=stat_send,
            recv_sem=stat_recv,
            device_id={"seq": to},
            device_id_type=MESH,
        ).start()
        return carry

    lax.fori_loop(1, n, send_stats, 0)
    home[me] = back[me]
    mine = pl.ds(pl.multiple_of(me * cols, cols), cols)
    home_stats[mine, :] = col_stats[mine, :]

    stat_all = pltpu.make_async_remote_copy(
        src_ref=col_stats.at[pl.ds(0, tokens - cols)],
        dst_ref=home_stats.at[pl.ds(0, tokens - cols)],
        send_sem=stat_send,
        recv_sem=stat_recv,
        device_id={"seq": peer(1)},
        device_id_type=MESH,
    )
    for chunk in range(chunks):
        for copy in chunk_copies(chunk):
            copy.wait_send()
    stat_all.wait()

    row_high, col_high = row_stats[...], home_stats[...]
    highest = jnp.maximum(row_high, col_high)
    row_factor = jnp.exp2((row_high - highest) * POWER)
    col_factor = jnp.exp2((col_high - highest) * POWER)
    row_total = pltpu.roll(row_high, HD - HEADS, 1)
    col_total = pltpu.roll(col_high, HD - HEADS, 1)
    total = row_total * row_factor + col_total * col_factor
    total = jnp.where(lane < HEADS, total, 1.0)
    row_factor = row_factor / total
    col_factor = col_factor / total

    for chunk in range(chunks):
        back_copies(chunk).wait()
        for sub in range(CHUNK_HEADS):
            head = chunk * CHUNK_HEADS + sub
            at = pl.ds(head * HD, HD)
            merged = row_out[:, at].astype(jnp.float32) * row_factor[:, head : head + 1]
            col_part = home[:, :, at].reshape(tokens, HD).astype(jnp.float32)
            merged = merged + col_part * col_factor[:, head : head + 1]
            out_ref[:, :, at] = merged.astype(jnp.bfloat16).reshape(n, cols, HD)


def local(query_vectors, key_vectors, value_vectors):
    n = lax.axis_size("seq")
    _, columns, width = query_vectors.shape
    cols = columns // n
    split = (n, cols, width)
    chunks = HEADS // CHUNK_HEADS
    vmem = pl.BlockSpec(memory_space=pltpu.VMEM)
    block = pltpu.VMEM(split, jnp.bfloat16)
    stats = pltpu.VMEM((columns, HD), jnp.float32)
    bias = pltpu.VMEM((columns, columns), jnp.float32)
    dma = pltpu.SemaphoreType.DMA
    finished = pl.pallas_call(
        functools.partial(kernel, n, cols),
        out_shape=jax.ShapeDtypeStruct(split, jnp.bfloat16),
        in_specs=[vmem] * 3,
        out_specs=vmem,
        scratch_shapes=[block] * 5
        + [pltpu.VMEM((columns, width), jnp.bfloat16)]
        + [stats] * 3
        + [bias] * 2
        + [dma((chunks, 3)), dma((chunks, 3)), dma((chunks,)), dma((chunks,)), dma, dma, dma((3,))],
        compiler_params=pltpu.CompilerParams(
            collective_id=0, has_side_effects=True, vmem_limit_bytes=40 * 2**20
        ),
        cost_estimate=pl.CostEstimate(
            flops=8 * columns * columns * width,
            bytes_accessed=8 * columns * width,
            transcendentals=2 * HEADS * columns * columns,
        ),
        name="strided_attention",
    )(
        query_vectors.reshape(split),
        key_vectors.reshape(split),
        value_vectors.reshape(split),
    )
    return finished.reshape(query_vectors.shape)


def solution(mesh):
    spec = P(("grp", "seq"), None, None)
    return jax.shard_map(
        local, mesh=mesh, in_specs=(spec, spec, spec), out_specs=spec, check_vma=False
    )
```

```python
import functools
import math

import jax
import jax.numpy as jnp
from jax import lax
from jax.experimental import pallas as pl
from jax.experimental.pallas import tpu as pltpu
from jax.sharding import PartitionSpec as P

HEADS = 16
HD = 128
FLOOR = -1e30
POWER = math.log2(math.e) / math.sqrt(HD)
CHUNK_HEADS = 4
MESH = pl.DeviceIdType.MESH


def attend(queries, keys, values, bias):
    scores = lax.dot_general(
        queries, keys, (((1,), (1,)), ((), ())), preferred_element_type=jnp.float32
    )
    scores = scores + bias
    high = jnp.max(scores, axis=1, keepdims=True)
    weights = jnp.exp2((scores - high) * POWER)
    total = jnp.sum(weights, axis=1, keepdims=True)
    out = jnp.dot(weights.astype(jnp.bfloat16), values, preferred_element_type=jnp.float32)
    return out, high, total


def kernel(
    n, cols,
    q_hbm, k_hbm, v_hbm, out_ref,
    q_ref, k_ref, v_ref, q_all, k_all, v_all, back, home, row_out, row_stats, col_stats, stats_out, stats_in, home_stats, row_bias, col_bias,
    send_sem, recv_sem, back_send, back_recv, stat_send, stat_recv, own_sem, load_sem,
):
    me = lax.axis_index("seq")
    width = CHUNK_HEADS * HD
    chunks = HEADS // CHUNK_HEADS
    tokens = n * cols
    forward = ((q_ref, q_all), (k_ref, k_all), (v_ref, v_all))

    def peer(step):
        return lax.rem(me + step, n)

    def far_first(turn):
        away = lax.div(turn + 1, 2)
        return peer(n // 2 + away * (2 * lax.rem(turn, 2) - 1))

    barrier = pltpu.get_barrier_semaphore()

    def greet(step, carry):
        pl.semaphore_signal(
            barrier, inc=1, device_id={"seq": peer(step)}, device_id_type=MESH
        )
        return carry

    lax.fori_loop(1, n, greet, 0)

    loads = [
        pltpu.make_async_copy(src, dst, load_sem.at[i])
        for i, (src, dst) in enumerate(((q_hbm, q_ref), (k_hbm, k_ref), (v_hbm, v_ref)))
    ]
    for copy in loads:
        copy.start()
    own = [
        pltpu.make_async_copy(src.at[me], dst.at[me], own_sem.at[i])
        for i, (src, dst) in enumerate(forward)
    ]

    index = lax.broadcasted_iota(jnp.int32, (tokens, tokens), 0)
    other = lax.broadcasted_iota(jnp.int32, (tokens, tokens), 1)
    row_bias[...] = jnp.where(other <= index, 0.0, FLOOR)
    same = lax.rem(index, cols) == lax.rem(other, cols)
    before = lax.div(other, cols) < lax.div(index, cols)
    col_bias[...] = jnp.where(same & before, 0.0, FLOOR)

    row_stats[...] = jnp.zeros_like(row_stats)
    col_stats[...] = jnp.zeros_like(col_stats)
    for load, copy in zip(loads, own):
        load.wait()
        copy.start()

    pl.semaphore_wait(barrier, n - 1)

    def lanes(chunk):
        return pl.ds(chunk * width, width)

    def send_chunk(chunk):
        def send(step, carry):
            to = far_first(step)
            for i, (src, dst) in enumerate(forward):
                pltpu.make_async_remote_copy(
                    src_ref=src.at[to, :, lanes(chunk)],
                    dst_ref=dst.at[me, :, lanes(chunk)],
                    send_sem=send_sem.at[chunk, i],
                    recv_sem=recv_sem.at[chunk, i],
                    device_id={"seq": to},
                    device_id_type=MESH,
                ).start()
            return carry

        lax.fori_loop(0, n - 1, send, 0)

    def chunk_copies(chunk):
        return [
            pltpu.make_async_remote_copy(
                src_ref=src.at[pl.ds(0, n - 1), :, lanes(chunk)],
                dst_ref=dst.at[pl.ds(0, n - 1), :, lanes(chunk)],
                send_sem=send_sem.at[chunk, i],
                recv_sem=recv_sem.at[chunk, i],
                device_id={"seq": peer(1)},
                device_id_type=MESH,
            )
            for i, (src, dst) in enumerate(forward)
        ]

    def back_copies(chunk):
        return pltpu.make_async_remote_copy(
            src_ref=back.at[pl.ds(0, n - 1), :, lanes(chunk)],
            dst_ref=home.at[pl.ds(0, n - 1), :, lanes(chunk)],
            send_sem=back_send.at[chunk],
            recv_sem=back_recv.at[chunk],
            device_id={"seq": peer(1)},
            device_id_type=MESH,
        )

    lane = lax.broadcasted_iota(jnp.int32, (tokens, HD), 1)

    def keep(stats, head, high, total):
        stats[...] = jnp.where(
            lane == head, high, jnp.where(lane == head + HEADS, total, stats[...])
        )

    def row_chunk(chunk):
        for sub in range(CHUNK_HEADS):
            head = chunk * CHUNK_HEADS + sub
            at = pl.ds(head * HD, HD)
            out, high, total = attend(
                q_ref[:, :, at].reshape(tokens, HD),
                k_ref[:, :, at].reshape(tokens, HD),
                v_ref[:, :, at].reshape(tokens, HD),
                row_bias[...],
            )
            row_out[:, at] = out.astype(jnp.bfloat16)
            keep(row_stats, head, high, total)

    def col_chunk(chunk):
        for sub in range(CHUNK_HEADS):
            head = chunk * CHUNK_HEADS + sub
            at = pl.ds(head * HD, HD)
            out, high, total = attend(
                q_all[:, :, at].reshape(tokens, HD),
                k_all[:, :, at].reshape(tokens, HD),
                v_all[:, :, at].reshape(tokens, HD),
                col_bias[...],
            )
            back[:, :, at] = out.astype(jnp.bfloat16).reshape(n, cols, HD)
            keep(col_stats, head, high, total)

    for chunk in range(chunks):
        send_chunk(chunk)

    def row_step(chunk, carry):
        row_chunk(chunk)
        return carry

    lax.fori_loop(0, chunks, row_step, 0)

    for copy in own:
        copy.wait()

    def col_step(chunk, carry):
        for copy in chunk_copies(chunk):
            copy.wait_recv()
        col_chunk(chunk)

        def send_back(step, inner):
            to = far_first(step)
            pltpu.make_async_remote_copy(
                src_ref=back.at[to, :, lanes(chunk)],
                dst_ref=home.at[me, :, lanes(chunk)],
                send_sem=back_send.at[chunk],
                recv_sem=back_recv.at[chunk],
                device_id={"seq": to},
                device_id_type=MESH,
            ).start()
            return inner

        lax.fori_loop(0, n - 1, send_back, 0)
        return carry

    lax.fori_loop(0, chunks, col_step, 0)


    wide = lax.broadcasted_iota(jnp.int32, (n, HD), 1)
    highs = jnp.zeros((n, HD), jnp.float32)
    totals = highs
    for column in range(cols):
        part = col_stats[pl.ds(column, n, stride=cols), :]
        here = lax.div(wide, HEADS) == column
        highs = jnp.where(here, pltpu.roll(part, column * HEADS, 1), highs)
        totals = jnp.where(here, pltpu.roll(part, (column - 1) * HEADS % HD, 1), totals)
    stats_out[:, 0, :] = highs
    stats_out[:, 1, :] = totals

    def send_stats(step, carry):
        to = far_first(step)
        pltpu.make_async_remote_copy(
            src_ref=stats_out.at[to],
            dst_ref=stats_in.at[me],
            send_sem=stat_send,
            recv_sem=stat_recv,
            device_id={"seq": to},
            device_id_type=MESH,
        ).start()
        return carry

    lax.fori_loop(0, n - 1, send_stats, 0)
    home[me] = back[me]
    stats_in[me] = stats_out[me]

    stat_all = pltpu.make_async_remote_copy(
        src_ref=stats_out.at[pl.ds(0, n - 1)],
        dst_ref=stats_in.at[pl.ds(0, n - 1)],
        send_sem=stat_send,
        recv_sem=stat_recv,
        device_id={"seq": peer(1)},
        device_id_type=MESH,
    )
    for chunk in range(chunks):
        for copy in chunk_copies(chunk):
            copy.wait_send()
    stat_all.wait()

    highs, totals = stats_in[:, 0, :], stats_in[:, 1, :]
    for column in range(cols):
        back_high = pltpu.roll(highs, -column * HEADS % HD, 1)
        back_total = pltpu.roll(totals, (1 - column) * HEADS % HD, 1)
        home_stats[pl.ds(column, n, stride=cols), :] = jnp.where(
            wide < HEADS, back_high, back_total
        )
    row_high, col_high = row_stats[...], home_stats[...]
    highest = jnp.maximum(row_high, col_high)
    row_factor = jnp.exp2((row_high - highest) * POWER)
    col_factor = jnp.exp2((col_high - highest) * POWER)
    row_total = pltpu.roll(row_high, HD - HEADS, 1)
    col_total = pltpu.roll(col_high, HD - HEADS, 1)
    total = row_total * row_factor + col_total * col_factor
    total = jnp.where(lane < HEADS, total, 1.0)
    row_factor = row_factor / total
    col_factor = col_factor / total

    for chunk in range(chunks):
        back_copies(chunk).wait()
        for sub in range(CHUNK_HEADS):
            head = chunk * CHUNK_HEADS + sub
            at = pl.ds(head * HD, HD)
            merged = row_out[:, at].astype(jnp.float32) * row_factor[:, head : head + 1]
            col_part = home[:, :, at].reshape(tokens, HD).astype(jnp.float32)
            merged = merged + col_part * col_factor[:, head : head + 1]
            out_ref[:, :, at] = merged.astype(jnp.bfloat16).reshape(n, cols, HD)


def local(query_vectors, key_vectors, value_vectors):
    n = lax.axis_size("seq")
    _, columns, width = query_vectors.shape
    cols = columns // n
    split = (n, cols, width)
    chunks = HEADS // CHUNK_HEADS
    vmem = pl.BlockSpec(memory_space=pltpu.VMEM)
    block = pltpu.VMEM(split, jnp.bfloat16)
    stats = pltpu.VMEM((columns, HD), jnp.float32)
    bias = pltpu.VMEM((columns, columns), jnp.float32)
    dma = pltpu.SemaphoreType.DMA
    finished = pl.pallas_call(
        functools.partial(kernel, n, cols),
        out_shape=jax.ShapeDtypeStruct(split, jnp.bfloat16),
        in_specs=[pl.BlockSpec(memory_space=pl.ANY)] * 3,
        out_specs=vmem,
        scratch_shapes=[block] * 8
        + [pltpu.VMEM((columns, width), jnp.bfloat16)]
        + [stats] * 2
        + [pltpu.VMEM((n, 2, HD), jnp.float32)] * 2
        + [stats]
        + [bias] * 2
        + [dma((chunks, 3)), dma((chunks, 3)), dma((chunks,)), dma((chunks,)), dma, dma, dma((3,)), dma((3,))],
        compiler_params=pltpu.CompilerParams(
            collective_id=0, has_side_effects=True, vmem_limit_bytes=56 * 2**20
        ),
        cost_estimate=pl.CostEstimate(
            flops=8 * columns * columns * width,
            bytes_accessed=8 * columns * width,
            transcendentals=2 * HEADS * columns * columns,
        ),
        name="strided_attention",
    )(
        query_vectors.reshape(split),
        key_vectors.reshape(split),
        value_vectors.reshape(split),
    )
    return finished.reshape(query_vectors.shape)


def solution(mesh):
    spec = P(("grp", "seq"), None, None)
    return jax.shard_map(
        local, mesh=mesh, in_specs=(spec, spec, spec), out_specs=spec, check_vma=False
    )
```

```python
import functools
import math

import jax
import jax.numpy as jnp
from jax import lax
from jax.experimental import pallas as pl
from jax.experimental.pallas import tpu as pltpu
from jax.sharding import PartitionSpec as P

HEADS = 16
HD = 128
FLOOR = -1e30
POWER = math.log2(math.e) / math.sqrt(HD)
CHUNK_HEADS = 8
CHUNKS = HEADS // CHUNK_HEADS
WIDTH = CHUNK_HEADS * HD
MESH = pl.DeviceIdType.MESH

ROLES = (
    (1, 0, 0x701F, 0xFE06), (15, 16, 0x1FFF, 0xFFF0), (27, 8, 0x03FF, 0xFFFE),
    (21, 24, 0x3FFF, 0xFFE0), (19, 4, 0x41FF, 0xFFFE), (17, 20, 0x7F00, 0xFE00),
    (30, 12, 0x0FFF, 0xFFFC), (29, 28, 0x701F, 0xFFFE), (11, 2, 0x7FFF, 0xFFFE),
    (2, 18, 0x1FE0, 0xFFC0), (5, 10, 0x07FF, 0xFFF8), (23, 26, 0x701F, 0xFF06),
    (22, 6, 0x03FF, 0xFFFE), (8, 22, 0x7FFF, 0xFFE0), (13, 14, 0x1FFF, 0xFFF0),
    (25, 30, 0x607F, 0xFFFE), (0, 1, 0x701F, 0xFE02), (24, 17, 0x0FF0, 0xFFE0),
    (28, 9, 0x03FF, 0xFFFE), (18, 25, 0x780F, 0xFFC0), (9, 5, 0x41FF, 0xFFFC),
    (25, 21, 0x1F80, 0xFF00), (12, 13, 0x07FF, 0xFFF0), (31, 29, 0x603F, 0xFFFE),
    (10, 3, 0x0007, 0x000E), (0, 19, 0x0FE0, 0xFFC0), (6, 11, 0x07FF, 0xFFF8),
    (22, 27, 0x7C00, 0xF800), (3, 7, 0x03FF, 0xFFFC), (20, 23, 0x0FFF, 0xFFE0),
    (14, 15, 0x1FFF, 0xFFF0), (24, 31, 0x700F, 0xFF06), (2, 1, 0x601F, 0xFE06),
    (18, 17, 0x07F0, 0xFFE0), (26, 9, 0x00FF, 0x01F8), (27, 25, 0x7C00, 0xF800),
    (17, 5, 0x00FF, 0xFFFE), (31, 21, 0x1FC0, 0xFE00), (16, 13, 0x07FF, 0xFFF0),
    (3, 29, 0x7C00, 0xF800), (12, 3, 0x0007, 0x000E), (1, 19, 0x0FE0, 0xFFC0),
    (5, 27, 0x7800, 0xF000), (0, 7, 0x001F, 0x01FC), (9, 23, 0x3E00, 0xFC00),
    (26, 31, 0x603F, 0xFE06), (7, 0, 0x0007, 0x000E), (23, 16, 0x0FE0, 0xFF00),
    (4, 8, 0x07FF, 0xFFF8), (28, 24, 0x7C00, 0xF800), (18, 4, 0x000F, 0x003E),
    (26, 20, 0x1FC0, 0xFE00), (29, 12, 0x0060, 0x00C0), (7, 28, 0x603F, 0xFFF0),
    (15, 2, 0x0007, 0x000E), (7, 18, 0x1FC0, 0xFF80), (10, 10, 0x07FF, 0xFFF0),
    (6, 26, 0x7800, 0xF000), (23, 6, 0x007F, 0x00F8), (19, 22, 0x3E00, 0xF800),
    (31, 14, 0x00C0, 0x0180), (4, 30, 0x7800, 0xF000), (4, 0, 0x0003, 0x0006),
    (20, 4, 0x000F, 0x001E), (19, 20, 0x0200, 0x0400), (30, 28, 0x0001, 0x0002),
    (8, 2, 0x0001, 0x0002), (29, 18, 0x0FE0, 0xFF00), (16, 26, 0x7800, 0xF000),
    (2, 6, 0x001F, 0x01F8), (13, 30, 0x6000, 0xC000), (6, 1, 0x0003, 0x0006),
    (8, 5, 0x000F, 0x001C), (12, 29, 0x7800, 0xF000), (13, 3, 0x0007, 0x000E),
    (10, 27, 0x7800, 0xF000), (1, 7, 0x001F, 0x01F8), (14, 31, 0x6000, 0xC000),
    (3, 1, 0x0001, 0x0002), (16, 5, 0x0007, 0x000E), (20, 29, 0x7000, 0xE000),
    (14, 3, 0x0007, 0x000E), (30, 27, 0x7000, 0xE000), (24, 7, 0x000F, 0x00F8),
    (21, 31, 0x4000, 0x8000), (5, 0, 0x0003, 0x0006), (21, 4, 0x000F, 0x001E),
    (9, 2, 0x0001, 0x0002), (15, 30, 0x6000, 0xC000),
)


def slots_of(n):
    taken = [0] * n
    seen = {}
    out = []
    for group, device, key_mask, query_mask in ROLES:
        before = seen.get(group, 0)
        seen[group] = before | query_mask
        out.append((group, device, taken[device], key_mask, query_mask, before & query_mask))
        taken[device] += 1
    return out, taken


def attend(queries, keys, values, bias, strict):
    scores = lax.dot_general(
        queries, keys, (((1,), (1,)), ((), ())), preferred_element_type=jnp.float32
    )
    scores = jnp.where(bias == 0.0, scores, FLOOR) if strict else scores + bias
    high = jnp.max(scores, axis=1, keepdims=True)
    weights = jnp.exp2((scores - high) * POWER)
    total = jnp.sum(weights, axis=1, keepdims=True)
    out = jnp.dot(weights.astype(jnp.bfloat16), values, preferred_element_type=jnp.float32)
    return out, high, total


def kernel(
    n, cols, slots,
    q_hbm, k_hbm, v_hbm, out_ref,
    q_ref, k_ref, v_ref, q_all, k_all, v_all, back, home, k_pair, v_pair, row_out,
    row_stats, pair_stats, col_stats, stats_out, stats_in, home_stats, row_bias, col_bias,
    load_sem, send_sem, recv_sem, back_send, back_recv, stat_send, stat_recv, pair_send, pair_recv,
):
    me = lax.axis_index("seq")
    layer, side = lax.div(me, 2), lax.rem(me, 2)
    tokens = n * cols
    layers = n // 2
    roles, taken = slots_of(n)
    sources = ((q_ref, q_all), (k_ref, k_all), (v_ref, v_all))

    def pick(values, index):
        out = index * 0
        for i, value in enumerate(values):
            if value:
                out = jnp.where(index == i, value, out)
        return out

    def when_count(values, index, act):
        chosen = pick(values, index)
        for value in sorted(set(values)):
            if value:
                pl.when(chosen == value)(functools.partial(act, value))

    def layer_bit(mask):
        return pick([mask >> i & 1 for i in range(layers)], layer)

    def table(slot, field, default=0):
        values = [default] * n
        for role in roles:
            if role[2] == slot:
                values[role[1]] = role[field]
        return values

    def lanes(chunk):
        return pl.ds(chunk * WIDTH, WIDTH)

    v_all[...] = jnp.zeros_like(v_all)
    home[...] = jnp.zeros_like(home)
    empty = lax.broadcasted_iota(jnp.int32, (n, 2, HD), 1)
    for part in range(2):
        stats_in[part] = jnp.where(empty == 0, FLOOR, 0.0)

    barrier = pltpu.get_barrier_semaphore()

    def greet(step, carry):
        pl.semaphore_signal(
            barrier, inc=1, device_id={"seq": lax.rem(me + step, n)}, device_id_type=MESH
        )
        return carry

    lax.fori_loop(1, n, greet, 0)

    loads = [
        pltpu.make_async_copy(src, dst, load_sem.at[i])
        for i, (src, dst) in enumerate(((q_hbm, q_ref), (k_hbm, k_ref), (v_hbm, v_ref)))
    ]
    for copy in loads:
        copy.start()

    index = lax.broadcasted_iota(jnp.int32, (tokens, tokens), 0)
    other = lax.broadcasted_iota(jnp.int32, (tokens, tokens), 1)
    row_bias[...] = jnp.where(other <= index, 0.0, FLOOR)
    index_layer = lax.div(index, 2 * cols)
    other_layer = lax.div(other, 2 * cols)
    below = (lax.rem(index, cols) == lax.rem(other, cols)) & (other_layer < index_layer)
    slot_group, slot_queries, slot_second = [], [], []
    for slot in range(slots):
        key_bits = pick(table(slot, 3), me)
        query_bits = pick(table(slot, 4), me)
        slot_group.append(pick(table(slot, 0), me))
        slot_queries.append(query_bits)
        slot_second.append(pick(table(slot, 5), me))
        allowed = (jnp.right_shift(query_bits, index_layer) & 1) * (
            jnp.right_shift(key_bits, other_layer) & 1
        )
        col_bias[slot] = jnp.where(below & (allowed == 1), 0.0, FLOOR)
    row_stats[...] = jnp.zeros_like(row_stats)
    pair_stats[...] = jnp.zeros_like(pair_stats)
    col_stats[...] = jnp.zeros_like(col_stats)
    for copy in loads:
        copy.wait()

    pl.semaphore_wait(barrier, n - 1)

    pairs = ((k_ref, k_pair), (v_ref, v_pair))
    pair_copies = [
        pltpu.make_async_remote_copy(
            src_ref=src, dst_ref=dst, send_sem=pair_send.at[i], recv_sem=pair_recv.at[i],
            device_id={"seq": lax.rem(me + 1, n)}, device_id_type=MESH,
        )
        for i, (src, dst) in enumerate(pairs)
    ]
    own_copies = [
        pltpu.make_async_copy(src, dst, pair_recv.at[i]) for i, (src, dst) in enumerate(pairs)
    ]

    def send_forward(chunk, carry):
        for group, device, slot, key_mask, query_mask, _ in roles:
            for wanted, arrays in ((key_mask, (1, 2)), (query_mask, (0,))):

                def go(group=group, device=device, slot=slot, arrays=arrays):
                    for i in arrays:
                        src, dst = sources[i]
                        pltpu.make_async_remote_copy(
                            src_ref=src.at[group, :, lanes(chunk)],
                            dst_ref=dst.at[slot, me, :, lanes(chunk)],
                            send_sem=send_sem.at[chunk, i],
                            recv_sem=recv_sem.at[slot, chunk, i],
                            device_id={"seq": me * 0 + device},
                            device_id_type=MESH,
                        ).start()

                pl.when((layer_bit(wanted) == 1) & (me != device))(go)
        return carry

    def own_forward(chunk, carry):
        for slot in range(slots):
            for field, arrays in ((3, (1, 2)), (4, (0,))):
                wanted = [
                    1 if mask >> (i // 2) & 1 else 0 for i, mask in enumerate(table(slot, field))
                ]

                def go(slot=slot, arrays=arrays):
                    for i in arrays:
                        src, dst = sources[i]
                        pltpu.make_async_copy(
                            src.at[slot_group[slot], :, lanes(chunk)],
                            dst.at[slot, me, :, lanes(chunk)],
                            recv_sem.at[slot, chunk, i],
                        ).start()

                pl.when(pick(wanted, me) == 1)(go)
        return carry

    def wait_forward(slot, chunk):
        for i, field in ((0, 4), (1, 3), (2, 3)):
            src, dst = sources[i]
            counts = [2 * mask.bit_count() for mask in table(slot, field)]

            def act(count, i=i, dst=dst):
                pltpu.make_async_copy(
                    dst.at[slot, pl.ds(0, count), :, lanes(chunk)],
                    dst.at[slot, pl.ds(0, count), :, lanes(chunk)],
                    recv_sem.at[slot, chunk, i],
                ).wait()

            when_count(counts, me, act)

    lane = lax.broadcasted_iota(jnp.int32, (tokens, HD), 1)

    def kept(stats, head, high, total):
        return jnp.where(lane == head, high, jnp.where(lane == head + HEADS, total, stats))

    def row_step(turn, carry):
        for sub in range(2):
            head = turn * 2 + sub
            at = pl.ds(pl.multiple_of(head * HD, HD), HD)
            out, high, total = attend(
                q_ref[:, :, at].reshape(tokens, HD),
                k_ref[:, :, at].reshape(tokens, HD),
                v_ref[:, :, at].reshape(tokens, HD),
                row_bias[...],
                False,
            )
            row_out[:, at] = out.astype(jnp.bfloat16)
            row_stats[...] = kept(row_stats[...], head, high, total)
        return carry

    def col_heads(slot, chunk):
        def step(turn, carry):
            for sub in range(2):
                head = chunk * CHUNK_HEADS + turn * 2 + sub
                at = pl.ds(pl.multiple_of(head * HD, HD), HD)
                out, high, total = attend(
                    q_all[slot, :, :, at].reshape(tokens, HD),
                    k_all[slot, :, :, at].reshape(tokens, HD),
                    v_all[slot, :, :, at].reshape(tokens, HD),
                    col_bias[slot],
                    True,
                )
                back[slot, :, :, at] = out.astype(jnp.bfloat16).reshape(n, cols, HD)
                col_stats[slot] = kept(col_stats[slot], head, high, total)
            return carry

        lax.fori_loop(0, CHUNK_HEADS // 2, step, 0)

    def each_row(slot, act):
        def step(turn, carry):
            row = lax.rem(me + turn, n)
            wanted = jnp.right_shift(slot_queries[slot], lax.div(row, 2)) & 1
            part = jnp.right_shift(slot_second[slot], lax.div(row, 2)) & 1
            pl.when((wanted == 1) & (turn > 0))(lambda: act(row, part, True))
            pl.when((wanted == 1) & (turn == 0))(lambda: act(row, part, False))
            return carry

        lax.fori_loop(0, n, step, 0)

    def send_back(slot, chunk):
        def act(row, part, far):
            src = back.at[slot, row, :, lanes(chunk)]
            dst = home.at[part, slot_group[slot], :, lanes(chunk)]
            if far:
                pltpu.make_async_remote_copy(
                    src_ref=src, dst_ref=dst,
                    send_sem=back_send.at[slot, chunk], recv_sem=back_recv.at[part, chunk],
                    device_id={"seq": row}, device_id_type=MESH,
                ).start()
            else:
                pltpu.make_async_copy(src, dst, back_recv.at[part, chunk]).start()

        each_row(slot, act)

    wide = lax.broadcasted_iota(jnp.int32, (n, HD), 1)

    def send_stats(slot):
        highs = jnp.zeros((n, HD), jnp.float32)
        totals = highs
        for column in range(cols):
            part = col_stats[slot, pl.ds(column, n, stride=cols), :]
            here = lax.div(wide, HEADS) == column
            highs = jnp.where(here, pltpu.roll(part, column * HEADS, 1), highs)
            totals = jnp.where(here, pltpu.roll(part, (column - 1) * HEADS % HD, 1), totals)
        stats_out[slot, :, 0, :] = highs
        stats_out[slot, :, 1, :] = totals

        def act(row, part, far):
            src = stats_out.at[slot, row]
            dst = stats_in.at[part, slot_group[slot]]
            if far:
                pltpu.make_async_remote_copy(
                    src_ref=src, dst_ref=dst,
                    send_sem=stat_send.at[slot], recv_sem=stat_recv.at[part],
                    device_id={"seq": row}, device_id_type=MESH,
                ).start()
            else:
                pltpu.make_async_copy(src, dst, stat_recv.at[part]).start()

        each_row(slot, act)

    lax.fori_loop(0, CHUNKS, send_forward, 0)
    lax.fori_loop(0, CHUNKS, own_forward, 0)

    @pl.when(side == 0)
    def _():
        for copy in pair_copies + own_copies:
            copy.start()

    lax.fori_loop(0, HEADS // 2, row_step, 0)

    for chunk in range(CHUNKS):
        for slot in range(slots):
            present = pick([1 if taken[i] > slot else 0 for i in range(n)], me) == 1

            @pl.when(present)
            def _(slot=slot, chunk=chunk):
                wait_forward(slot, chunk)
                col_heads(slot, chunk)
                send_back(slot, chunk)
                if chunk == CHUNKS - 1:
                    send_stats(slot)

    for i, (src, dst) in enumerate(pairs):
        pltpu.make_async_copy(src, dst, pair_recv.at[i]).wait()

    def pair_step(head, carry):
        at = pl.ds(pl.multiple_of(head * HD, HD), HD)
        product = q_ref[:, :, at].reshape(tokens, HD).astype(jnp.float32) * k_pair[
            :, :, at
        ].reshape(tokens, HD).astype(jnp.float32)
        high = jnp.sum(product, axis=1, keepdims=True)
        pair_stats[...] = kept(pair_stats[...], head, high, 1.0)
        return carry

    lax.fori_loop(0, HEADS, pair_step, 0)

    parts = [[0] * layers for _ in range(2)]
    for _, _, _, _, query_mask, second in roles:
        for i in range(layers):
            if query_mask >> i & 1:
                parts[second >> i & 1][i] += 1

    for part in range(2):

        def act(count, part=part):
            pltpu.make_async_copy(
                stats_in.at[part, pl.ds(0, count)], stats_in.at[part, pl.ds(0, count)],
                stat_recv.at[part],
            ).wait()

        when_count(parts[part], layer, act)

    def merged_stats(part):
        highs, totals = stats_in[part, :, 0, :], stats_in[part, :, 1, :]
        for column in range(cols):
            back_high = pltpu.roll(highs, -column * HEADS % HD, 1)
            back_total = pltpu.roll(totals, (1 - column) * HEADS % HD, 1)
            home_stats[pl.ds(column, n, stride=cols), :] = jnp.where(
                wide < HEADS, back_high, back_total
            )
        return home_stats[...]

    offset = jnp.where(side == 1, 0.0, FLOOR)
    pair_high = jnp.where(lane < HEADS, pair_stats[...] + offset, pair_stats[...])
    terms = [row_stats[...], merged_stats(0), merged_stats(1), pair_high]
    highest = functools.reduce(jnp.maximum, terms)
    factors = [jnp.exp2((term - highest) * POWER) for term in terms]
    total = sum(pltpu.roll(term, HD - HEADS, 1) * f for term, f in zip(terms, factors))
    total = jnp.where(lane < HEADS, total, 1.0)
    factors = [f / total for f in factors]

    for chunk in range(CHUNKS):
        for part in range(2):

            def act(count, part=part, chunk=chunk):
                pltpu.make_async_copy(
                    home.at[part, pl.ds(0, count), :, lanes(chunk)],
                    home.at[part, pl.ds(0, count), :, lanes(chunk)],
                    back_recv.at[part, chunk],
                ).wait()

            when_count(parts[part], layer, act)
        for sub in range(CHUNK_HEADS):
            head = chunk * CHUNK_HEADS + sub
            at = pl.ds(head * HD, HD)
            blocks = (
                row_out[:, at],
                home[0, :, :, at].reshape(tokens, HD),
                home[1, :, :, at].reshape(tokens, HD),
                v_pair[:, :, at].reshape(tokens, HD),
            )
            merged = sum(
                block.astype(jnp.float32) * f[:, head : head + 1]
                for block, f in zip(blocks, factors)
            )
            out_ref[:, :, at] = merged.astype(jnp.bfloat16).reshape(n, cols, HD)

    sent_keys = [0] * n
    sent_queries = [0] * n
    for _, device, _, key_mask, query_mask, _ in roles:
        for i in range(n):
            if i != device:
                sent_keys[i] += key_mask >> (i // 2) & 1
                sent_queries[i] += query_mask >> (i // 2) & 1
    for chunk in range(CHUNKS):
        for i, counts in ((0, sent_queries), (1, sent_keys), (2, sent_keys)):
            src, dst = sources[i]

            def act(count, i=i, dst=dst, chunk=chunk):
                whole, rest = count // n, count % n
                for size in [n] * whole + [rest] * (rest > 0):
                    pltpu.make_async_remote_copy(
                        src_ref=dst.at[0, pl.ds(0, size), :, lanes(chunk)],
                        dst_ref=dst.at[0, pl.ds(0, size), :, lanes(chunk)],
                        send_sem=send_sem.at[chunk, i], recv_sem=recv_sem.at[0, chunk, i],
                        device_id={"seq": lax.rem(me + 1, n)}, device_id_type=MESH,
                    ).wait_send()

            when_count(counts, me, act)
    for slot in range(slots):
        counts = [
            2 * mask.bit_count() - (mask >> (i // 2) & 1)
            for i, mask in enumerate(table(slot, 4))
        ]

        def act(count, slot=slot):
            for chunk in range(CHUNKS):
                pltpu.make_async_remote_copy(
                    src_ref=back.at[slot, pl.ds(0, count), :, lanes(chunk)],
                    dst_ref=back.at[slot, pl.ds(0, count), :, lanes(chunk)],
                    send_sem=back_send.at[slot, chunk], recv_sem=back_recv.at[0, chunk],
                    device_id={"seq": lax.rem(me + 1, n)}, device_id_type=MESH,
                ).wait_send()
            pltpu.make_async_remote_copy(
                src_ref=stats_out.at[slot, pl.ds(0, count)],
                dst_ref=stats_out.at[slot, pl.ds(0, count)],
                send_sem=stat_send.at[slot], recv_sem=stat_recv.at[0],
                device_id={"seq": lax.rem(me + 1, n)}, device_id_type=MESH,
            ).wait_send()

        when_count(counts, me, act)

    @pl.when(side == 0)
    def _():
        for copy in pair_copies:
            copy.wait_send()


def local(query_vectors, key_vectors, value_vectors):
    n = lax.axis_size("seq")
    _, columns, width = query_vectors.shape
    cols = columns // n
    split = (n, cols, width)
    slots = max(slots_of(n)[1])
    block = pltpu.VMEM(split, jnp.bfloat16)
    blocks = pltpu.VMEM((slots,) + split, jnp.bfloat16)
    stats = pltpu.VMEM((columns, HD), jnp.float32)
    dma = pltpu.SemaphoreType.DMA
    finished = pl.pallas_call(
        functools.partial(kernel, n, cols, slots),
        out_shape=jax.ShapeDtypeStruct(split, jnp.bfloat16),
        in_specs=[pl.BlockSpec(memory_space=pl.ANY)] * 3,
        out_specs=pl.BlockSpec(memory_space=pltpu.VMEM),
        scratch_shapes=[block] * 3
        + [blocks] * 4
        + [pltpu.VMEM((2,) + split, jnp.bfloat16)]
        + [block] * 2
        + [pltpu.VMEM((columns, width), jnp.bfloat16)]
        + [stats] * 2
        + [pltpu.VMEM((slots, columns, HD), jnp.float32)]
        + [pltpu.VMEM((slots, n, 2, HD), jnp.float32), pltpu.VMEM((2, n, 2, HD), jnp.float32)]
        + [stats]
        + [pltpu.VMEM((columns, columns), jnp.float32)]
        + [pltpu.VMEM((slots, columns, columns), jnp.float32)]
        + [dma((3,)), dma((CHUNKS, 3)), dma((slots, CHUNKS, 3))]
        + [dma((slots, CHUNKS)), dma((2, CHUNKS)), dma((slots,)), dma((2,)), dma((2,)), dma((2,))],
        compiler_params=pltpu.CompilerParams(
            collective_id=0, has_side_effects=True, vmem_limit_bytes=56 * 2**20
        ),
        cost_estimate=pl.CostEstimate(
            flops=16 * columns * columns * width,
            bytes_accessed=8 * columns * width,
            transcendentals=4 * HEADS * columns * columns,
        ),
        name="strided_attention",
    )(
        query_vectors.reshape(split),
        key_vectors.reshape(split),
        value_vectors.reshape(split),
    )
    return finished.reshape(query_vectors.shape)


def solution(mesh):
    spec = P(("grp", "seq"), None, None)
    return jax.shard_map(
        local, mesh=mesh, in_specs=(spec, spec, spec), out_specs=spec, check_vma=False
    )
```

```python
import functools
import math

import jax
import jax.numpy as jnp
from jax import lax
from jax.experimental import pallas as pl
from jax.experimental.pallas import tpu as pltpu
from jax.sharding import PartitionSpec as P

HEADS = 16
HD = 128
FLOOR = -1e30
POWER = math.log2(math.e) / math.sqrt(HD)
CHUNK_HEADS = 4
CHUNKS = HEADS // CHUNK_HEADS
WIDTH = CHUNK_HEADS * HD
MESH = pl.DeviceIdType.MESH

ROLES = (
    (4, 0, 0x703F, 0xFE06), (22, 16, 0x07F0, 0xFFC0), (5, 8, 0x00FF, 0x01F8),
    (22, 24, 0x780F, 0xFFC0), (8, 4, 0x41FF, 0xFFFC), (2, 20, 0x1FC0, 0xFE00),
    (14, 12, 0x07FF, 0xFFF0), (24, 28, 0x781F, 0xFF82), (17, 2, 0x41FF, 0xFFFE),
    (28, 18, 0x0FE0, 0xFFC0), (6, 10, 0x07FF, 0xFFFC), (19, 26, 0x7C00, 0xF800),
    (10, 6, 0x03FF, 0xFFF8), (7, 22, 0x7FFF, 0xFFF8), (16, 14, 0x1FFF, 0xFFF0),
    (29, 30, 0x603F, 0xFE06), (1, 1, 0x603F, 0xFE06), (23, 17, 0x0FFF, 0xFFF0),
    (18, 9, 0x03FF, 0xFFF0), (21, 25, 0x7FFF, 0xFFC0), (9, 5, 0x41FF, 0xFFFC),
    (1, 21, 0x1FC0, 0xFE00), (12, 13, 0x07FF, 0xFFF0), (27, 29, 0x701F, 0xFF86),
    (13, 3, 0x0007, 0x000E), (0, 19, 0x0FE0, 0xFFC0), (30, 11, 0x07FF, 0xFFF8),
    (11, 27, 0x7800, 0xF000), (1, 7, 0x00FF, 0x01F8), (8, 23, 0x3E00, 0xFC00),
    (15, 15, 0x1FFF, 0xFFF0), (31, 31, 0x607F, 0xFFFE), (2, 1, 0x603F, 0xFE06),
    (24, 17, 0x07E0, 0xFFC0), (19, 9, 0x03FF, 0xFFF0), (18, 25, 0x7C00, 0xF800),
    (21, 5, 0x001F, 0x003E), (3, 21, 0x1FC0, 0xFE00), (13, 13, 0x07FF, 0xFFF0),
    (28, 29, 0x701F, 0xFF02), (14, 3, 0x0007, 0x000E), (4, 19, 0x0FC0, 0xFE00),
    (13, 27, 0x7800, 0xF000), (3, 7, 0x00FF, 0x01F8), (17, 23, 0x3E00, 0xFC00),
    (26, 15, 0x0FF0, 0xFFE0), (15, 31, 0x6000, 0xC000), (3, 0, 0x603F, 0xFE06),
    (25, 16, 0x0FE0, 0xFFC0), (29, 8, 0x00FF, 0x01F8), (10, 24, 0x7C00, 0xF800),
    (24, 4, 0x001F, 0x007C), (29, 20, 0x1FC0, 0xFE00), (20, 12, 0x07FF, 0xFFF0),
    (25, 28, 0x701F, 0xFFE2), (11, 2, 0x0007, 0x000E), (5, 18, 0x1FC0, 0xFE00),
    (11, 10, 0x07FF, 0xFFF0), (12, 26, 0x7800, 0xF000), (2, 6, 0x00FF, 0x01F8),
    (9, 22, 0x3E00, 0xFC00), (31, 14, 0x0180, 0x0300), (30, 30, 0x0003, 0x0006),
    (7, 0, 0x0003, 0x0006), (27, 16, 0x0FE0, 0xFFC0), (19, 4, 0x0007, 0x000E),
    (26, 28, 0x700F, 0xFF82), (12, 2, 0x0007, 0x000E), (30, 26, 0x7800, 0xF000),
    (0, 6, 0x001F, 0x01FC), (5, 1, 0x603F, 0xFE06), (4, 9, 0x00FF, 0x01F8),
    (22, 5, 0x001F, 0x003E), (31, 21, 0x1F80, 0xFC00), (16, 3, 0x0007, 0x000E),
    (14, 27, 0x7800, 0xF000), (28, 7, 0x001F, 0x00FC), (16, 31, 0x6000, 0xC000),
    (0, 1, 0x701F, 0xFE02), (25, 5, 0x000F, 0x001C), (10, 3, 0x0003, 0x0006),
    (20, 27, 0x7800, 0xF000), (27, 7, 0x001F, 0x0078), (6, 0, 0x0001, 0x0002),
    (20, 4, 0x0007, 0x000E), (6, 28, 0x7800, 0xF000), (15, 2, 0x0007, 0x000E),
    (26, 6, 0x000F, 0x007C), (23, 4, 0x0007, 0x000E), (9, 2, 0x0001, 0x0002),
    (18, 5, 0x0007, 0x000E), (8, 3, 0x0001, 0x0002), (23, 27, 0x7000, 0xE000),
)


def slots_of(n):
    taken = [0] * n
    seen = {}
    out = []
    for group, device, key_mask, query_mask in ROLES:
        before = seen.get(group, 0)
        seen[group] = before | query_mask
        out.append((group, device, taken[device], key_mask, query_mask, before & query_mask))
        taken[device] += 1
    return out, taken


def attend(queries, keys, values, bias, strict):
    scores = lax.dot_general(
        queries, keys, (((1,), (1,)), ((), ())), preferred_element_type=jnp.float32
    )
    scores = jnp.where(bias == 0.0, scores, FLOOR) if strict else scores + bias
    high = jnp.max(scores, axis=1, keepdims=True)
    weights = jnp.exp2((scores - high) * POWER)
    total = jnp.sum(weights, axis=1, keepdims=True)
    out = jnp.dot(weights.astype(jnp.bfloat16), values, preferred_element_type=jnp.float32)
    return out, high, total


def kernel(
    n, cols, slots,
    q_hbm, k_hbm, v_hbm, out_ref,
    q_ref, k_ref, v_ref, q_all, k_all, v_all, back, home, k_pair, v_pair, row_out,
    row_stats, pair_stats, col_stats, stats_out, stats_in, home_stats, row_bias, col_bias,
    load_sem, send_sem, recv_sem, back_send, back_recv, stat_send, stat_recv, pair_send, pair_recv,
):
    me = lax.axis_index("seq")
    layer, side = lax.div(me, 2), lax.rem(me, 2)
    tokens = n * cols
    layers = n // 2
    roles, taken = slots_of(n)
    sources = ((q_ref, q_all), (k_ref, k_all), (v_ref, v_all))

    def pick(values, index):
        out = index * 0
        for i, value in enumerate(values):
            if value:
                out = jnp.where(index == i, value, out)
        return out

    def when_count(values, index, act):
        chosen = pick(values, index)
        for value in sorted(set(values)):
            if value:
                pl.when(chosen == value)(functools.partial(act, value))

    def layer_bit(mask):
        return pick([mask >> i & 1 for i in range(layers)], layer)

    def table(slot, field, default=0):
        values = [default] * n
        for role in roles:
            if role[2] == slot:
                values[role[1]] = role[field]
        return values

    def lanes(chunk):
        return pl.ds(chunk * WIDTH, WIDTH)

    v_all[...] = jnp.zeros_like(v_all)
    home[...] = jnp.zeros_like(home)
    empty = lax.broadcasted_iota(jnp.int32, (n, 2, HD), 1)
    for part in range(2):
        stats_in[part] = jnp.where(empty == 0, FLOOR, 0.0)

    barrier = pltpu.get_barrier_semaphore()

    def greet(step, carry):
        pl.semaphore_signal(
            barrier, inc=1, device_id={"seq": lax.rem(me + step, n)}, device_id_type=MESH
        )
        return carry

    lax.fori_loop(1, n, greet, 0)

    loads = [
        pltpu.make_async_copy(src, dst, load_sem.at[i])
        for i, (src, dst) in enumerate(((q_hbm, q_ref), (k_hbm, k_ref), (v_hbm, v_ref)))
    ]
    for copy in loads:
        copy.start()

    index = lax.broadcasted_iota(jnp.int32, (tokens, tokens), 0)
    other = lax.broadcasted_iota(jnp.int32, (tokens, tokens), 1)
    row_bias[...] = jnp.where(other <= index, 0.0, FLOOR)
    index_layer = lax.div(index, 2 * cols)
    other_layer = lax.div(other, 2 * cols)
    below = (lax.rem(index, cols) == lax.rem(other, cols)) & (other_layer < index_layer)
    slot_group, slot_queries, slot_second = [], [], []
    for slot in range(slots):
        key_bits = pick(table(slot, 3), me)
        query_bits = pick(table(slot, 4), me)
        slot_group.append(pick(table(slot, 0), me))
        slot_queries.append(query_bits)
        slot_second.append(pick(table(slot, 5), me))
        allowed = (jnp.right_shift(query_bits, index_layer) & 1) * (
            jnp.right_shift(key_bits, other_layer) & 1
        )
        col_bias[slot] = jnp.where(below & (allowed == 1), 0.0, FLOOR)
    row_stats[...] = jnp.zeros_like(row_stats)
    pair_stats[...] = jnp.zeros_like(pair_stats)
    col_stats[...] = jnp.zeros_like(col_stats)
    for copy in loads:
        copy.wait()

    pl.semaphore_wait(barrier, n - 1)

    pairs = ((k_ref, k_pair), (v_ref, v_pair))
    pair_copies = [
        pltpu.make_async_remote_copy(
            src_ref=src, dst_ref=dst, send_sem=pair_send.at[i], recv_sem=pair_recv.at[i],
            device_id={"seq": lax.rem(me + 1, n)}, device_id_type=MESH,
        )
        for i, (src, dst) in enumerate(pairs)
    ]
    own_copies = [
        pltpu.make_async_copy(src, dst, pair_recv.at[i]) for i, (src, dst) in enumerate(pairs)
    ]

    def send_forward(chunk, carry):
        for group, device, slot, key_mask, query_mask, _ in roles:
            for wanted, arrays in ((key_mask, (1, 2)), (query_mask, (0,))):

                def go(group=group, device=device, slot=slot, arrays=arrays):
                    for i in arrays:
                        src, dst = sources[i]
                        pltpu.make_async_remote_copy(
                            src_ref=src.at[group, :, lanes(chunk)],
                            dst_ref=dst.at[slot, me, :, lanes(chunk)],
                            send_sem=send_sem.at[chunk, i],
                            recv_sem=recv_sem.at[slot, chunk, i],
                            device_id={"seq": me * 0 + device},
                            device_id_type=MESH,
                        ).start()

                pl.when((layer_bit(wanted) == 1) & (me != device))(go)
        return carry

    def own_forward(chunk, carry):
        for slot in range(slots):
            for field, arrays in ((3, (1, 2)), (4, (0,))):
                wanted = [
                    1 if mask >> (i // 2) & 1 else 0 for i, mask in enumerate(table(slot, field))
                ]

                def go(slot=slot, arrays=arrays):
                    for i in arrays:
                        src, dst = sources[i]
                        pltpu.make_async_copy(
                            src.at[slot_group[slot], :, lanes(chunk)],
                            dst.at[slot, me, :, lanes(chunk)],
                            recv_sem.at[slot, chunk, i],
                        ).start()

                pl.when(pick(wanted, me) == 1)(go)
        return carry

    def wait_forward(slot, chunk):
        for i, field in ((0, 4), (1, 3), (2, 3)):
            src, dst = sources[i]
            counts = [2 * mask.bit_count() for mask in table(slot, field)]

            def act(count, i=i, dst=dst):
                pltpu.make_async_copy(
                    dst.at[slot, pl.ds(0, count), :, lanes(chunk)],
                    dst.at[slot, pl.ds(0, count), :, lanes(chunk)],
                    recv_sem.at[slot, chunk, i],
                ).wait()

            when_count(counts, me, act)

    lane = lax.broadcasted_iota(jnp.int32, (tokens, HD), 1)

    def kept(stats, head, high, total):
        return jnp.where(lane == head, high, jnp.where(lane == head + HEADS, total, stats))

    def row_step(turn, carry):
        for sub in range(2):
            head = turn * 2 + sub
            at = pl.ds(pl.multiple_of(head * HD, HD), HD)
            out, high, total = attend(
                q_ref[:, :, at].reshape(tokens, HD),
                k_ref[:, :, at].reshape(tokens, HD),
                v_ref[:, :, at].reshape(tokens, HD),
                row_bias[...],
                False,
            )
            row_out[:, at] = out.astype(jnp.bfloat16)
            row_stats[...] = kept(row_stats[...], head, high, total)
        return carry

    def col_heads(slot, chunk):
        def step(turn, carry):
            for sub in range(2):
                head = chunk * CHUNK_HEADS + turn * 2 + sub
                at = pl.ds(pl.multiple_of(head * HD, HD), HD)
                out, high, total = attend(
                    q_all[slot, :, :, at].reshape(tokens, HD),
                    k_all[slot, :, :, at].reshape(tokens, HD),
                    v_all[slot, :, :, at].reshape(tokens, HD),
                    col_bias[slot],
                    True,
                )
                back[slot, :, :, at] = out.astype(jnp.bfloat16).reshape(n, cols, HD)
                col_stats[slot] = kept(col_stats[slot], head, high, total)
            return carry

        lax.fori_loop(0, CHUNK_HEADS // 2, step, 0)

    def each_row(slot, act):
        def step(turn, carry):
            row = lax.rem(me + turn, n)
            wanted = jnp.right_shift(slot_queries[slot], lax.div(row, 2)) & 1
            part = jnp.right_shift(slot_second[slot], lax.div(row, 2)) & 1
            pl.when((wanted == 1) & (turn > 0))(lambda: act(row, part, True))
            pl.when((wanted == 1) & (turn == 0))(lambda: act(row, part, False))
            return carry

        lax.fori_loop(0, n, step, 0)

    def send_back(slot, chunk):
        def act(row, part, far):
            src = back.at[slot, row, :, lanes(chunk)]
            dst = home.at[part, slot_group[slot], :, lanes(chunk)]
            if far:
                pltpu.make_async_remote_copy(
                    src_ref=src, dst_ref=dst,
                    send_sem=back_send.at[slot, chunk], recv_sem=back_recv.at[part, chunk],
                    device_id={"seq": row}, device_id_type=MESH,
                ).start()
            else:
                pltpu.make_async_copy(src, dst, back_recv.at[part, chunk]).start()

        each_row(slot, act)

    wide = lax.broadcasted_iota(jnp.int32, (n, HD), 1)

    def send_stats(slot):
        highs = jnp.zeros((n, HD), jnp.float32)
        totals = highs
        for column in range(cols):
            part = col_stats[slot, pl.ds(column, n, stride=cols), :]
            here = lax.div(wide, HEADS) == column
            highs = jnp.where(here, pltpu.roll(part, column * HEADS, 1), highs)
            totals = jnp.where(here, pltpu.roll(part, (column - 1) * HEADS % HD, 1), totals)
        stats_out[slot, :, 0, :] = highs
        stats_out[slot, :, 1, :] = totals

        def act(row, part, far):
            src = stats_out.at[slot, row]
            dst = stats_in.at[part, slot_group[slot]]
            if far:
                pltpu.make_async_remote_copy(
                    src_ref=src, dst_ref=dst,
                    send_sem=stat_send.at[slot], recv_sem=stat_recv.at[part],
                    device_id={"seq": row}, device_id_type=MESH,
                ).start()
            else:
                pltpu.make_async_copy(src, dst, stat_recv.at[part]).start()

        each_row(slot, act)

    lax.fori_loop(0, CHUNKS, send_forward, 0)
    lax.fori_loop(0, CHUNKS, own_forward, 0)

    @pl.when(side == 0)
    def _():
        for copy in pair_copies + own_copies:
            copy.start()

    lax.fori_loop(0, HEADS // 2, row_step, 0)

    for chunk in range(CHUNKS):
        for slot in range(slots):
            present = pick([1 if taken[i] > slot else 0 for i in range(n)], me) == 1

            @pl.when(present)
            def _(slot=slot, chunk=chunk):
                wait_forward(slot, chunk)
                col_heads(slot, chunk)
                send_back(slot, chunk)
                if chunk == CHUNKS - 1:
                    send_stats(slot)

    for i, (src, dst) in enumerate(pairs):
        pltpu.make_async_copy(src, dst, pair_recv.at[i]).wait()

    def pair_step(head, carry):
        at = pl.ds(pl.multiple_of(head * HD, HD), HD)
        product = q_ref[:, :, at].reshape(tokens, HD).astype(jnp.float32) * k_pair[
            :, :, at
        ].reshape(tokens, HD).astype(jnp.float32)
        high = jnp.sum(product, axis=1, keepdims=True)
        pair_stats[...] = kept(pair_stats[...], head, high, 1.0)
        return carry

    lax.fori_loop(0, HEADS, pair_step, 0)

    parts = [[0] * layers for _ in range(2)]
    for _, _, _, _, query_mask, second in roles:
        for i in range(layers):
            if query_mask >> i & 1:
                parts[second >> i & 1][i] += 1

    for part in range(2):

        def act(count, part=part):
            pltpu.make_async_copy(
                stats_in.at[part, pl.ds(0, count)], stats_in.at[part, pl.ds(0, count)],
                stat_recv.at[part],
            ).wait()

        when_count(parts[part], layer, act)

    def merged_stats(part):
        highs, totals = stats_in[part, :, 0, :], stats_in[part, :, 1, :]
        for column in range(cols):
            back_high = pltpu.roll(highs, -column * HEADS % HD, 1)
            back_total = pltpu.roll(totals, (1 - column) * HEADS % HD, 1)
            home_stats[pl.ds(column, n, stride=cols), :] = jnp.where(
                wide < HEADS, back_high, back_total
            )
        return home_stats[...]

    offset = jnp.where(side == 1, 0.0, FLOOR)
    pair_high = jnp.where(lane < HEADS, pair_stats[...] + offset, pair_stats[...])
    terms = [row_stats[...], merged_stats(0), merged_stats(1), pair_high]
    highest = functools.reduce(jnp.maximum, terms)
    factors = [jnp.exp2((term - highest) * POWER) for term in terms]
    total = sum(pltpu.roll(term, HD - HEADS, 1) * f for term, f in zip(terms, factors))
    total = jnp.where(lane < HEADS, total, 1.0)
    factors = [f / total for f in factors]

    for chunk in range(CHUNKS):
        for part in range(2):

            def act(count, part=part, chunk=chunk):
                pltpu.make_async_copy(
                    home.at[part, pl.ds(0, count), :, lanes(chunk)],
                    home.at[part, pl.ds(0, count), :, lanes(chunk)],
                    back_recv.at[part, chunk],
                ).wait()

            when_count(parts[part], layer, act)
        for sub in range(CHUNK_HEADS):
            head = chunk * CHUNK_HEADS + sub
            at = pl.ds(head * HD, HD)
            blocks = (
                row_out[:, at],
                home[0, :, :, at].reshape(tokens, HD),
                home[1, :, :, at].reshape(tokens, HD),
                v_pair[:, :, at].reshape(tokens, HD),
            )
            merged = sum(
                block.astype(jnp.float32) * f[:, head : head + 1]
                for block, f in zip(blocks, factors)
            )
            out_ref[:, :, at] = merged.astype(jnp.bfloat16).reshape(n, cols, HD)

    sent_keys = [0] * n
    sent_queries = [0] * n
    for _, device, _, key_mask, query_mask, _ in roles:
        for i in range(n):
            if i != device:
                sent_keys[i] += key_mask >> (i // 2) & 1
                sent_queries[i] += query_mask >> (i // 2) & 1
    for chunk in range(CHUNKS):
        for i, counts in ((0, sent_queries), (1, sent_keys), (2, sent_keys)):
            src, dst = sources[i]

            def act(count, i=i, dst=dst, chunk=chunk):
                whole, rest = count // n, count % n
                for size in [n] * whole + [rest] * (rest > 0):
                    pltpu.make_async_remote_copy(
                        src_ref=dst.at[0, pl.ds(0, size), :, lanes(chunk)],
                        dst_ref=dst.at[0, pl.ds(0, size), :, lanes(chunk)],
                        send_sem=send_sem.at[chunk, i], recv_sem=recv_sem.at[0, chunk, i],
                        device_id={"seq": lax.rem(me + 1, n)}, device_id_type=MESH,
                    ).wait_send()

            when_count(counts, me, act)
    for slot in range(slots):
        counts = [
            2 * mask.bit_count() - (mask >> (i // 2) & 1)
            for i, mask in enumerate(table(slot, 4))
        ]

        def act(count, slot=slot):
            for chunk in range(CHUNKS):
                pltpu.make_async_remote_copy(
                    src_ref=back.at[slot, pl.ds(0, count), :, lanes(chunk)],
                    dst_ref=back.at[slot, pl.ds(0, count), :, lanes(chunk)],
                    send_sem=back_send.at[slot, chunk], recv_sem=back_recv.at[0, chunk],
                    device_id={"seq": lax.rem(me + 1, n)}, device_id_type=MESH,
                ).wait_send()
            pltpu.make_async_remote_copy(
                src_ref=stats_out.at[slot, pl.ds(0, count)],
                dst_ref=stats_out.at[slot, pl.ds(0, count)],
                send_sem=stat_send.at[slot], recv_sem=stat_recv.at[0],
                device_id={"seq": lax.rem(me + 1, n)}, device_id_type=MESH,
            ).wait_send()

        when_count(counts, me, act)

    @pl.when(side == 0)
    def _():
        for copy in pair_copies:
            copy.wait_send()


def local(query_vectors, key_vectors, value_vectors):
    n = lax.axis_size("seq")
    _, columns, width = query_vectors.shape
    cols = columns // n
    split = (n, cols, width)
    slots = max(slots_of(n)[1])
    block = pltpu.VMEM(split, jnp.bfloat16)
    blocks = pltpu.VMEM((slots,) + split, jnp.bfloat16)
    stats = pltpu.VMEM((columns, HD), jnp.float32)
    dma = pltpu.SemaphoreType.DMA
    finished = pl.pallas_call(
        functools.partial(kernel, n, cols, slots),
        out_shape=jax.ShapeDtypeStruct(split, jnp.bfloat16),
        in_specs=[pl.BlockSpec(memory_space=pl.ANY)] * 3,
        out_specs=pl.BlockSpec(memory_space=pltpu.VMEM),
        scratch_shapes=[block] * 3
        + [blocks] * 4
        + [pltpu.VMEM((2,) + split, jnp.bfloat16)]
        + [block] * 2
        + [pltpu.VMEM((columns, width), jnp.bfloat16)]
        + [stats] * 2
        + [pltpu.VMEM((slots, columns, HD), jnp.float32)]
        + [pltpu.VMEM((slots, n, 2, HD), jnp.float32), pltpu.VMEM((2, n, 2, HD), jnp.float32)]
        + [stats]
        + [pltpu.VMEM((columns, columns), jnp.float32)]
        + [pltpu.VMEM((slots, columns, columns), jnp.float32)]
        + [dma((3,)), dma((CHUNKS, 3)), dma((slots, CHUNKS, 3))]
        + [dma((slots, CHUNKS)), dma((2, CHUNKS)), dma((slots,)), dma((2,)), dma((2,)), dma((2,))],
        compiler_params=pltpu.CompilerParams(
            collective_id=0, has_side_effects=True, vmem_limit_bytes=56 * 2**20
        ),
        cost_estimate=pl.CostEstimate(
            flops=16 * columns * columns * width,
            bytes_accessed=8 * columns * width,
            transcendentals=4 * HEADS * columns * columns,
        ),
        name="strided_attention",
    )(
        query_vectors.reshape(split),
        key_vectors.reshape(split),
        value_vectors.reshape(split),
    )
    return finished.reshape(query_vectors.shape)


def solution(mesh):
    spec = P(("grp", "seq"), None, None)
    return jax.shard_map(
        local, mesh=mesh, in_specs=(spec, spec, spec), out_specs=spec, check_vma=False
    )
```

```python
import functools
import math

import jax
import jax.numpy as jnp
from jax import lax
from jax.experimental import pallas as pl
from jax.experimental.pallas import tpu as pltpu
from jax.sharding import PartitionSpec as P

HEADS = 16
HD = 128
FLOOR = -1e30
POWER = math.log2(math.e) / math.sqrt(HD)
CHUNK_HEADS = 4
CHUNKS = HEADS // CHUNK_HEADS
WIDTH = CHUNK_HEADS * HD
MESH = pl.DeviceIdType.MESH

ROLES = (
    (0, 0, 0x701F, 0xFE02), (24, 16, 0x0FF0, 0xFFE0), (27, 8, 0x03FF, 0xFFFE),
    (21, 24, 0x3FFF, 0xFFE0), (19, 4, 0x41FF, 0xFFFE), (31, 20, 0x1FC0, 0xFE00),
    (30, 12, 0x0FFF, 0xFFFC), (31, 28, 0x603F, 0xFFFE), (11, 2, 0x7FFF, 0xFFFE),
    (2, 18, 0x1FE0, 0xFFC0), (10, 10, 0x07FF, 0xFFF0), (23, 26, 0x701F, 0xFF06),
    (3, 6, 0x03FF, 0xFFFC), (8, 22, 0x7FFF, 0xFFE0), (14, 14, 0x1FFF, 0xFFF0),
    (25, 30, 0x607F, 0xFFFE), (1, 1, 0x701F, 0xFE06), (15, 17, 0x1FFF, 0xFFF0),
    (4, 9, 0x07FF, 0xFFF8), (18, 25, 0x780F, 0xFFC0), (9, 5, 0x41FF, 0xFFFC),
    (17, 21, 0x7F00, 0xFE00), (16, 13, 0x07FF, 0xFFF0), (29, 29, 0x701F, 0xFFFE),
    (12, 3, 0x0007, 0x000E), (1, 19, 0x0FE0, 0xFFC0), (5, 11, 0x07FF, 0xFFF8),
    (22, 27, 0x7C00, 0xF800), (22, 7, 0x03FF, 0xFFFE), (20, 23, 0x0FFF, 0xFFE0),
    (13, 15, 0x1FFF, 0xFFF0), (26, 31, 0x603F, 0xFE06), (2, 1, 0x601F, 0xFE06),
    (18, 17, 0x07F0, 0xFFE0), (26, 9, 0x00FF, 0x01F8), (27, 25, 0x7C00, 0xF800),
    (17, 5, 0x00FF, 0xFFFE), (26, 21, 0x1FC0, 0xFE00), (29, 13, 0x0060, 0x00C0),
    (7, 29, 0x603F, 0xFFF0), (14, 3, 0x0007, 0x000E), (7, 19, 0x1FC0, 0xFF80),
    (6, 11, 0x07FF, 0xFFF8), (5, 27, 0x7800, 0xF000), (23, 7, 0x007F, 0x00F8),
    (9, 23, 0x3E00, 0xFC00), (24, 31, 0x700F, 0xFF06), (7, 0, 0x0007, 0x000E),
    (23, 16, 0x0FE0, 0xFF00), (28, 8, 0x03FF, 0xFFFE), (28, 24, 0x7C00, 0xF800),
    (18, 4, 0x000F, 0x003E), (25, 20, 0x1F80, 0xFF00), (12, 12, 0x07FF, 0xFFF0),
    (3, 28, 0x7C00, 0xF800), (10, 2, 0x0007, 0x000E), (0, 18, 0x0FE0, 0xFFC0),
    (10, 26, 0x7800, 0xF000), (0, 6, 0x001F, 0x01FC), (31, 14, 0x00C0, 0x0180),
    (13, 30, 0x6000, 0xC000), (4, 0, 0x0003, 0x0006), (20, 4, 0x000F, 0x001E),
    (12, 28, 0x7800, 0xF000), (13, 2, 0x0007, 0x000E), (30, 26, 0x7000, 0xE000),
    (1, 6, 0x001F, 0x01F8), (14, 30, 0x6000, 0xC000), (5, 1, 0x0003, 0x0006),
    (8, 5, 0x000F, 0x001C), (19, 21, 0x0200, 0x0400), (30, 29, 0x0001, 0x0002),
    (15, 3, 0x0007, 0x000E), (29, 19, 0x0FE0, 0xFF00), (6, 27, 0x7800, 0xF000),
    (2, 7, 0x001F, 0x01F8), (19, 23, 0x3E00, 0xF800), (4, 31, 0x7800, 0xF000),
    (6, 1, 0x0003, 0x0006), (16, 5, 0x0007, 0x000E), (8, 3, 0x0001, 0x0002),
    (16, 27, 0x7800, 0xF000), (24, 7, 0x000F, 0x00F8), (15, 31, 0x6000, 0xC000),
    (3, 0, 0x0001, 0x0002), (21, 4, 0x000F, 0x001E), (20, 28, 0x7000, 0xE000),
    (9, 2, 0x0001, 0x0002), (21, 30, 0x4000, 0x8000),
)


def slots_of(n):
    taken = [0] * n
    seen = {}
    out = []
    for group, device, key_mask, query_mask in ROLES:
        before = seen.get(group, 0)
        seen[group] = before | query_mask
        out.append((group, device, taken[device], key_mask, query_mask, before & query_mask))
        taken[device] += 1
    return out, taken


def attend(queries, keys, values, bias, strict):
    scores = lax.dot_general(
        queries, keys, (((1,), (1,)), ((), ())), preferred_element_type=jnp.float32
    )
    scores = jnp.where(bias == 0.0, scores, FLOOR) if strict else scores + bias
    high = jnp.max(scores, axis=1, keepdims=True)
    weights = jnp.exp2((scores - high) * POWER)
    total = jnp.sum(weights, axis=1, keepdims=True)
    out = jnp.dot(weights.astype(jnp.bfloat16), values, preferred_element_type=jnp.float32)
    return out, high, total


def kernel(
    n, cols, slots,
    q_hbm, k_hbm, v_hbm, out_ref,
    q_ref, k_ref, v_ref, q_all, k_all, v_all, back, home, k_pair, v_pair, row_out,
    row_stats, pair_stats, col_stats, stats_out, stats_in, home_stats, row_bias, col_bias,
    load_sem, send_sem, recv_sem, back_send, back_recv, stat_send, stat_recv, pair_send, pair_recv,
):
    me = lax.axis_index("seq")
    layer, side = lax.div(me, 2), lax.rem(me, 2)
    tokens = n * cols
    layers = n // 2
    roles, taken = slots_of(n)
    sources = ((q_ref, q_all), (k_ref, k_all), (v_ref, v_all))

    def pick(values, index):
        out = index * 0
        for i, value in enumerate(values):
            if value:
                out = jnp.where(index == i, value, out)
        return out

    def when_count(values, index, act):
        chosen = pick(values, index)
        for value in sorted(set(values)):
            if value:
                pl.when(chosen == value)(functools.partial(act, value))

    def layer_bit(mask):
        return pick([mask >> i & 1 for i in range(layers)], layer)

    def table(slot, field, default=0):
        values = [default] * n
        for role in roles:
            if role[2] == slot:
                values[role[1]] = role[field]
        return values

    def lanes(chunk):
        return pl.ds(chunk * WIDTH, WIDTH)

    v_all[...] = jnp.zeros_like(v_all)
    home[...] = jnp.zeros_like(home)
    empty = lax.broadcasted_iota(jnp.int32, (n, 2, HD), 1)
    for part in range(2):
        stats_in[part] = jnp.where(empty == 0, FLOOR, 0.0)

    barrier = pltpu.get_barrier_semaphore()

    def greet(step, carry):
        pl.semaphore_signal(
            barrier, inc=1, device_id={"seq": lax.rem(me + step, n)}, device_id_type=MESH
        )
        return carry

    lax.fori_loop(1, n, greet, 0)

    loads = [
        pltpu.make_async_copy(src, dst, load_sem.at[i])
        for i, (src, dst) in enumerate(((q_hbm, q_ref), (k_hbm, k_ref), (v_hbm, v_ref)))
    ]
    for copy in loads:
        copy.start()

    index = lax.broadcasted_iota(jnp.int32, (tokens, tokens), 0)
    other = lax.broadcasted_iota(jnp.int32, (tokens, tokens), 1)
    row_bias[...] = jnp.where(other <= index, 0.0, FLOOR)
    index_layer = lax.div(index, 2 * cols)
    other_layer = lax.div(other, 2 * cols)
    below = (lax.rem(index, cols) == lax.rem(other, cols)) & (other_layer < index_layer)
    slot_group, slot_queries, slot_second = [], [], []
    for slot in range(slots):
        key_bits = pick(table(slot, 3), me)
        query_bits = pick(table(slot, 4), me)
        slot_group.append(pick(table(slot, 0), me))
        slot_queries.append(query_bits)
        slot_second.append(pick(table(slot, 5), me))
        allowed = (jnp.right_shift(query_bits, index_layer) & 1) * (
            jnp.right_shift(key_bits, other_layer) & 1
        )
        col_bias[slot] = jnp.where(below & (allowed == 1), 0.0, FLOOR)
    row_stats[...] = jnp.zeros_like(row_stats)
    pair_stats[...] = jnp.zeros_like(pair_stats)
    col_stats[...] = jnp.zeros_like(col_stats)
    for copy in loads:
        copy.wait()

    pl.semaphore_wait(barrier, n - 1)

    pairs = ((k_ref, k_pair), (v_ref, v_pair))
    pair_copies = [
        pltpu.make_async_remote_copy(
            src_ref=src, dst_ref=dst, send_sem=pair_send.at[i], recv_sem=pair_recv.at[i],
            device_id={"seq": lax.rem(me + 1, n)}, device_id_type=MESH,
        )
        for i, (src, dst) in enumerate(pairs)
    ]
    own_copies = [
        pltpu.make_async_copy(src, dst, pair_recv.at[i]) for i, (src, dst) in enumerate(pairs)
    ]

    def send_forward(chunk, carry):
        for group, device, slot, key_mask, query_mask, _ in roles:
            for wanted, arrays in ((key_mask, (1, 2)), (query_mask, (0,))):

                def go(group=group, device=device, slot=slot, arrays=arrays):
                    for i in arrays:
                        src, dst = sources[i]
                        pltpu.make_async_remote_copy(
                            src_ref=src.at[group, :, lanes(chunk)],
                            dst_ref=dst.at[slot, me, :, lanes(chunk)],
                            send_sem=send_sem.at[chunk, i],
                            recv_sem=recv_sem.at[slot, chunk, i],
                            device_id={"seq": me * 0 + device},
                            device_id_type=MESH,
                        ).start()

                pl.when((layer_bit(wanted) == 1) & (me != device))(go)
        return carry

    def own_forward(chunk, carry):
        for slot in range(slots):
            for field, arrays in ((3, (1, 2)), (4, (0,))):
                wanted = [
                    1 if mask >> (i // 2) & 1 else 0 for i, mask in enumerate(table(slot, field))
                ]

                def go(slot=slot, arrays=arrays):
                    for i in arrays:
                        src, dst = sources[i]
                        pltpu.make_async_copy(
                            src.at[slot_group[slot], :, lanes(chunk)],
                            dst.at[slot, me, :, lanes(chunk)],
                            recv_sem.at[slot, chunk, i],
                        ).start()

                pl.when(pick(wanted, me) == 1)(go)
        return carry

    def wait_forward(slot, chunk):
        for i, field in ((0, 4), (1, 3), (2, 3)):
            src, dst = sources[i]
            counts = [2 * mask.bit_count() for mask in table(slot, field)]

            def act(count, i=i, dst=dst):
                pltpu.make_async_copy(
                    dst.at[slot, pl.ds(0, count), :, lanes(chunk)],
                    dst.at[slot, pl.ds(0, count), :, lanes(chunk)],
                    recv_sem.at[slot, chunk, i],
                ).wait()

            when_count(counts, me, act)

    lane = lax.broadcasted_iota(jnp.int32, (tokens, HD), 1)

    def kept(stats, head, high, total):
        return jnp.where(lane == head, high, jnp.where(lane == head + HEADS, total, stats))

    def row_step(turn, carry):
        for sub in range(2):
            head = turn * 2 + sub
            at = pl.ds(pl.multiple_of(head * HD, HD), HD)
            out, high, total = attend(
                q_ref[:, :, at].reshape(tokens, HD),
                k_ref[:, :, at].reshape(tokens, HD),
                v_ref[:, :, at].reshape(tokens, HD),
                row_bias[...],
                False,
            )
            row_out[:, at] = out.astype(jnp.bfloat16)
            row_stats[...] = kept(row_stats[...], head, high, total)
        return carry

    def col_heads(slot, chunk):
        def step(turn, carry):
            for sub in range(2):
                head = chunk * CHUNK_HEADS + turn * 2 + sub
                at = pl.ds(pl.multiple_of(head * HD, HD), HD)
                out, high, total = attend(
                    q_all[slot, :, :, at].reshape(tokens, HD),
                    k_all[slot, :, :, at].reshape(tokens, HD),
                    v_all[slot, :, :, at].reshape(tokens, HD),
                    col_bias[slot],
                    True,
                )
                back[slot, :, :, at] = out.astype(jnp.bfloat16).reshape(n, cols, HD)
                col_stats[slot] = kept(col_stats[slot], head, high, total)
            return carry

        lax.fori_loop(0, CHUNK_HEADS // 2, step, 0)

    def each_row(slot, act):
        def step(turn, carry):
            row = lax.rem(me + turn, n)
            wanted = jnp.right_shift(slot_queries[slot], lax.div(row, 2)) & 1
            part = jnp.right_shift(slot_second[slot], lax.div(row, 2)) & 1
            pl.when((wanted == 1) & (turn > 0))(lambda: act(row, part, True))
            pl.when((wanted == 1) & (turn == 0))(lambda: act(row, part, False))
            return carry

        lax.fori_loop(0, n, step, 0)

    def send_back(slot, chunk):
        def act(row, part, far):
            src = back.at[slot, row, :, lanes(chunk)]
            dst = home.at[part, slot_group[slot], :, lanes(chunk)]
            if far:
                pltpu.make_async_remote_copy(
                    src_ref=src, dst_ref=dst,
                    send_sem=back_send.at[slot, chunk], recv_sem=back_recv.at[part, chunk],
                    device_id={"seq": row}, device_id_type=MESH,
                ).start()
            else:
                pltpu.make_async_copy(src, dst, back_recv.at[part, chunk]).start()

        each_row(slot, act)

    wide = lax.broadcasted_iota(jnp.int32, (n, HD), 1)

    def send_stats(slot):
        highs = jnp.zeros((n, HD), jnp.float32)
        totals = highs
        for column in range(cols):
            part = col_stats[slot, pl.ds(column, n, stride=cols), :]
            here = lax.div(wide, HEADS) == column
            highs = jnp.where(here, pltpu.roll(part, column * HEADS, 1), highs)
            totals = jnp.where(here, pltpu.roll(part, (column - 1) * HEADS % HD, 1), totals)
        stats_out[slot, :, 0, :] = highs
        stats_out[slot, :, 1, :] = totals

        def act(row, part, far):
            src = stats_out.at[slot, row]
            dst = stats_in.at[part, slot_group[slot]]
            if far:
                pltpu.make_async_remote_copy(
                    src_ref=src, dst_ref=dst,
                    send_sem=stat_send.at[slot], recv_sem=stat_recv.at[part],
                    device_id={"seq": row}, device_id_type=MESH,
                ).start()
            else:
                pltpu.make_async_copy(src, dst, stat_recv.at[part]).start()

        each_row(slot, act)

    lax.fori_loop(0, CHUNKS, send_forward, 0)
    lax.fori_loop(0, CHUNKS, own_forward, 0)

    @pl.when(side == 0)
    def _():
        for copy in pair_copies + own_copies:
            copy.start()

    lax.fori_loop(0, HEADS // 2, row_step, 0)

    for chunk in range(CHUNKS):
        for slot in range(slots):
            present = pick([1 if taken[i] > slot else 0 for i in range(n)], me) == 1

            @pl.when(present)
            def _(slot=slot, chunk=chunk):
                wait_forward(slot, chunk)
                col_heads(slot, chunk)
                send_back(slot, chunk)
                if chunk == CHUNKS - 1:
                    send_stats(slot)

    for i, (src, dst) in enumerate(pairs):
        pltpu.make_async_copy(src, dst, pair_recv.at[i]).wait()

    def pair_step(head, carry):
        at = pl.ds(pl.multiple_of(head * HD, HD), HD)
        product = q_ref[:, :, at].reshape(tokens, HD).astype(jnp.float32) * k_pair[
            :, :, at
        ].reshape(tokens, HD).astype(jnp.float32)
        high = jnp.sum(product, axis=1, keepdims=True)
        pair_stats[...] = kept(pair_stats[...], head, high, 1.0)
        return carry

    lax.fori_loop(0, HEADS, pair_step, 0)

    parts = [[0] * layers for _ in range(2)]
    for _, _, _, _, query_mask, second in roles:
        for i in range(layers):
            if query_mask >> i & 1:
                parts[second >> i & 1][i] += 1

    for part in range(2):

        def act(count, part=part):
            pltpu.make_async_copy(
                stats_in.at[part, pl.ds(0, count)], stats_in.at[part, pl.ds(0, count)],
                stat_recv.at[part],
            ).wait()

        when_count(parts[part], layer, act)

    def merged_stats(part):
        highs, totals = stats_in[part, :, 0, :], stats_in[part, :, 1, :]
        for column in range(cols):
            back_high = pltpu.roll(highs, -column * HEADS % HD, 1)
            back_total = pltpu.roll(totals, (1 - column) * HEADS % HD, 1)
            home_stats[pl.ds(column, n, stride=cols), :] = jnp.where(
                wide < HEADS, back_high, back_total
            )
        return home_stats[...]

    offset = jnp.where(side == 1, 0.0, FLOOR)
    pair_high = jnp.where(lane < HEADS, pair_stats[...] + offset, pair_stats[...])
    terms = [row_stats[...], merged_stats(0), merged_stats(1), pair_high]
    highest = functools.reduce(jnp.maximum, terms)
    factors = [jnp.exp2((term - highest) * POWER) for term in terms]
    total = sum(pltpu.roll(term, HD - HEADS, 1) * f for term, f in zip(terms, factors))
    total = jnp.where(lane < HEADS, total, 1.0)
    factors = [f / total for f in factors]

    for chunk in range(CHUNKS):
        for part in range(2):

            def act(count, part=part, chunk=chunk):
                pltpu.make_async_copy(
                    home.at[part, pl.ds(0, count), :, lanes(chunk)],
                    home.at[part, pl.ds(0, count), :, lanes(chunk)],
                    back_recv.at[part, chunk],
                ).wait()

            when_count(parts[part], layer, act)
        for sub in range(CHUNK_HEADS):
            head = chunk * CHUNK_HEADS + sub
            at = pl.ds(head * HD, HD)
            blocks = (
                row_out[:, at],
                home[0, :, :, at].reshape(tokens, HD),
                home[1, :, :, at].reshape(tokens, HD),
                v_pair[:, :, at].reshape(tokens, HD),
            )
            merged = sum(
                block.astype(jnp.float32) * f[:, head : head + 1]
                for block, f in zip(blocks, factors)
            )
            out_ref[:, :, at] = merged.astype(jnp.bfloat16).reshape(n, cols, HD)

    sent_keys = [0] * n
    sent_queries = [0] * n
    for _, device, _, key_mask, query_mask, _ in roles:
        for i in range(n):
            if i != device:
                sent_keys[i] += key_mask >> (i // 2) & 1
                sent_queries[i] += query_mask >> (i // 2) & 1
    for chunk in range(CHUNKS):
        for i, counts in ((0, sent_queries), (1, sent_keys), (2, sent_keys)):
            src, dst = sources[i]

            def act(count, i=i, dst=dst, chunk=chunk):
                whole, rest = count // n, count % n
                for size in [n] * whole + [rest] * (rest > 0):
                    pltpu.make_async_remote_copy(
                        src_ref=dst.at[0, pl.ds(0, size), :, lanes(chunk)],
                        dst_ref=dst.at[0, pl.ds(0, size), :, lanes(chunk)],
                        send_sem=send_sem.at[chunk, i], recv_sem=recv_sem.at[0, chunk, i],
                        device_id={"seq": lax.rem(me + 1, n)}, device_id_type=MESH,
                    ).wait_send()

            when_count(counts, me, act)
    for slot in range(slots):
        counts = [
            2 * mask.bit_count() - (mask >> (i // 2) & 1)
            for i, mask in enumerate(table(slot, 4))
        ]

        def act(count, slot=slot):
            for chunk in range(CHUNKS):
                pltpu.make_async_remote_copy(
                    src_ref=back.at[slot, pl.ds(0, count), :, lanes(chunk)],
                    dst_ref=back.at[slot, pl.ds(0, count), :, lanes(chunk)],
                    send_sem=back_send.at[slot, chunk], recv_sem=back_recv.at[0, chunk],
                    device_id={"seq": lax.rem(me + 1, n)}, device_id_type=MESH,
                ).wait_send()
            pltpu.make_async_remote_copy(
                src_ref=stats_out.at[slot, pl.ds(0, count)],
                dst_ref=stats_out.at[slot, pl.ds(0, count)],
                send_sem=stat_send.at[slot], recv_sem=stat_recv.at[0],
                device_id={"seq": lax.rem(me + 1, n)}, device_id_type=MESH,
            ).wait_send()

        when_count(counts, me, act)

    @pl.when(side == 0)
    def _():
        for copy in pair_copies:
            copy.wait_send()


def local(query_vectors, key_vectors, value_vectors):
    n = lax.axis_size("seq")
    _, columns, width = query_vectors.shape
    cols = columns // n
    split = (n, cols, width)
    slots = max(slots_of(n)[1])
    block = pltpu.VMEM(split, jnp.bfloat16)
    blocks = pltpu.VMEM((slots,) + split, jnp.bfloat16)
    stats = pltpu.VMEM((columns, HD), jnp.float32)
    dma = pltpu.SemaphoreType.DMA
    finished = pl.pallas_call(
        functools.partial(kernel, n, cols, slots),
        out_shape=jax.ShapeDtypeStruct(split, jnp.bfloat16),
        in_specs=[pl.BlockSpec(memory_space=pl.ANY)] * 3,
        out_specs=pl.BlockSpec(memory_space=pltpu.VMEM),
        scratch_shapes=[block] * 3
        + [blocks] * 4
        + [pltpu.VMEM((2,) + split, jnp.bfloat16)]
        + [block] * 2
        + [pltpu.VMEM((columns, width), jnp.bfloat16)]
        + [stats] * 2
        + [pltpu.VMEM((slots, columns, HD), jnp.float32)]
        + [pltpu.VMEM((slots, n, 2, HD), jnp.float32), pltpu.VMEM((2, n, 2, HD), jnp.float32)]
        + [stats]
        + [pltpu.VMEM((columns, columns), jnp.float32)]
        + [pltpu.VMEM((slots, columns, columns), jnp.float32)]
        + [dma((3,)), dma((CHUNKS, 3)), dma((slots, CHUNKS, 3))]
        + [dma((slots, CHUNKS)), dma((2, CHUNKS)), dma((slots,)), dma((2,)), dma((2,)), dma((2,))],
        compiler_params=pltpu.CompilerParams(
            collective_id=0, has_side_effects=True, vmem_limit_bytes=56 * 2**20
        ),
        cost_estimate=pl.CostEstimate(
            flops=16 * columns * columns * width,
            bytes_accessed=8 * columns * width,
            transcendentals=4 * HEADS * columns * columns,
        ),
        name="strided_attention",
    )(
        query_vectors.reshape(split),
        key_vectors.reshape(split),
        value_vectors.reshape(split),
    )
    return finished.reshape(query_vectors.shape)


def solution(mesh):
    spec = P(("grp", "seq"), None, None)
    return jax.shard_map(
        local, mesh=mesh, in_specs=(spec, spec, spec), out_specs=spec, check_vma=False
    )
```
